32 devices in a mesh: seq: 8 (over z, y), tp: 4 (over x, core).
Axes of the slice: x: 2, y: 2, z: 4, core: 2. Of those that a mesh axis runs over, the one named last changes fastest.
Arguments:
- hidden_in: bfloat16 [16, 1024, 2048], P('seq', None, 'tp'), may hold values from -6 to 6
- cotangent: bfloat16 [16, 1024, 2048], P('seq', None, 'tp'), may hold values from -6 to 6
- token_mask: int32 [16, 1024], P('seq'), may hold values 0 or 1
- w_qkv: bfloat16 [2048, 3, 16, 128], P(None, None, 'tp'), may hold values from -0.125 to 0.125
- w_out: bfloat16 [16, 128, 2048], P('tp'), may hold values from -0.125 to 0.125
- time_bias: float32 [16, 16, 16], P('tp'), may hold values from -2 to 252
Outputs:
- grad_input: bfloat16 [16, 1024, 2048], P('seq', None, 'tp')
- grad_qkv: float32 [2048, 3, 16, 128], P('seq', None, 'tp')
- grad_out: float32 [16, 128, 2048], P('tp', None, 'seq')
The draws below stay inside these ranges and needn't reach their ends.
All inputs are finite; a program needn't handle non-finite values. No bound on the sum of `token_mask` on one device may be relied on, other than what follows from the above.
Results may differ from the reference program's by a relative error of at most 0.012.
The reference program's roundings to bfloat16 on the way count: a program that leaves them out, or rounds other values in their place, can miss the bound.
Values may be sent and summed in bfloat16 or wider, within the bound.
No kernel may reach another device: no remote copies, remote signals or barrier semaphores. Data moves between devices by JAX's collectives and lax.ppermute only.
A program may use at most 192 MiB of HBM per device.

```python
import math
import jax
import jax.numpy as jnp
from jax import lax

D = 2048
HEADS = 16
HD = 128
FRAMES = 16
POS = 1024
TOKENS = 16384


def draw_time_bias(key, part):
    key = jax.random.fold_in(key, 7)
    keys = jax.random.split(key, 1)
    base = jax.random.uniform(keys[0], (HEADS, FRAMES, FRAMES), jnp.float32, -2.0, 2.0)
    return base


def plant(entries, rng, smallest, high):
    dims = entries.shape
    spot = [jax.random.randint(jax.random.fold_in(rng, axis), (), 0, dims[axis]) for axis in range(len(dims))]
    entries = entries.at[tuple(spot)].set(smallest)
    longest = dims.index(max(dims))
    spot[longest] = (spot[longest] + 1) % dims[longest]
    return entries.at[tuple(spot)].set(high)


def spiked(drawn, stream_key, source, target, blocks, factor):
    def block_of(axis_at):
        return (jnp.arange(drawn.shape[axis_at]) // (drawn.shape[axis_at] // blocks)).reshape((-1,) + (1,) * (drawn.ndim - 1 - axis_at))

    first = jax.random.permutation(stream_key, blocks)[block_of(target)]
    far = (block_of(target) + blocks // 2) % blocks
    return jnp.where((block_of(source) == first) | (block_of(source) == far), factor * drawn, drawn)


def block_levels(stream_key, shape, cuts, least, top_value):
    def one(axis_at, shards_of):
        draws = jax.random.uniform(jax.random.fold_in(jax.random.fold_in(stream_key, 6), axis_at), (shards_of,), jnp.float32, least / len(cuts), top_value / len(cuts))
        return jnp.repeat(jnp.exp(draws), shape[axis_at] // shards_of).reshape((-1,) + (1,) * (len(shape) - axis_at - 1))

    loudness = one(*cuts[0])
    for cut in cuts[1:]:
        loudness = loudness * one(*cut)
    return loudness


def noise(own_key, extent, deviation, reach, cuts=(), held_as=jnp.bfloat16):
    level = block_levels(own_key, extent, cuts, -0.22, 0.18) if cuts else 1.0
    result = jax.random.normal(own_key, extent, jnp.float32) * deviation * level
    return jnp.minimum(jnp.maximum(result, -reach), reach).astype(held_as)


def bell_draw_with(key, shape, scale, most, cuts, heavy, dtype=jnp.bfloat16):
    array = scale * jax.random.normal(key, shape, jnp.float32)
    if cuts:
        array = array * block_levels(key, shape, cuts, -0.22, 0.18)
    return jnp.clip(spiked(array, jax.random.fold_in(key, 3), *heavy), -most, most).astype(dtype)


def setup_inputs(seed: int = 0) -> dict:
    streams_of = jax.random.split(jax.random.key(seed), 7)
    return {
        "hidden_in": bell_draw_with(streams_of[0], (FRAMES, POS, D), 1.0, 6.0, ((0, 8), (2, 4)), (1, 2, 4, 2.0)),
        "cotangent": bell_draw_with(streams_of[1], (FRAMES, POS, D), 1.0, 6.0, ((0, 8), (2, 4)), (1, 2, 4, 2.0)),
        "token_mask": plant((jax.random.randint(streams_of[2], (FRAMES, POS), 0, 2) < 1).astype(jnp.int32), jax.random.fold_in(streams_of[2], 1), 0, 1),
        "w_qkv": noise(streams_of[3], (D, 3, HEADS, HD), D ** -0.5, 0.125, ((2, 4),)),
        "w_out": noise(streams_of[4], (HEADS, HD, D), (HEADS * HD) ** -0.5, 0.125, ((0, 4),)),
        "time_bias": draw_time_bias(jax.random.fold_in(streams_of[6], 71), 0),
    }


def reference(hidden_in, cotangent, token_mask, w_qkv, w_out, time_bias):
    scale = 1.0 / math.sqrt(HD)
    masked = cotangent * token_mask[:, :, None].astype(jnp.bfloat16)
    flat_in = hidden_in.reshape(TOKENS, D)
    flat_grad = masked.reshape(TOKENS, D)
    head_w = jnp.moveaxis(w_qkv, 2, 0)

    def step(total, pieces):
        proj, out_w, bias = pieces
        proj_flat = proj.reshape(D, 3 * HD)
        qkv = jnp.dot(flat_in, proj_flat, preferred_element_type=jnp.float32).astype(jnp.bfloat16)
        qkv = qkv.reshape(FRAMES, POS, 3, HD).astype(jnp.float32)
        query, keys, values = (qkv[:, :, 0], qkv[:, :, 1], qkv[:, :, 2])
        scores = jnp.einsum('fpd,gpd->pfg', query, keys) * scale + bias[None]
        probs = jax.nn.softmax(scores, axis=-1)
        probs_low = probs.astype(jnp.bfloat16).astype(jnp.float32)
        attn = jnp.einsum('pfg,gpd->fpd', probs_low, values).astype(jnp.bfloat16)
        d_attn = jnp.dot(flat_grad, out_w.T, preferred_element_type=jnp.float32).astype(jnp.bfloat16)
        out_grad = jnp.dot(attn.reshape(TOKENS, HD).T, flat_grad, preferred_element_type=jnp.float32)
        d_attn4 = d_attn.reshape(FRAMES, POS, HD).astype(jnp.float32)
        d_values = jnp.einsum('pfg,fpd->gpd', probs_low, d_attn4)
        d_probs = jnp.einsum('fpd,gpd->pfg', d_attn4, values)
        d_scores = probs * (d_probs - lax.optimization_barrier(jnp.sum(probs * d_probs, axis=-1, keepdims=True)))
        d_scores = d_scores.astype(jnp.bfloat16).astype(jnp.float32)
        d_query = jnp.einsum('pfg,gpd->fpd', d_scores, keys) * scale
        d_keys = jnp.einsum('pfg,fpd->gpd', d_scores, query) * scale
        d_qkv = jnp.stack([d_query, d_keys, d_values], axis=2).astype(jnp.bfloat16).reshape(TOKENS, 3 * HD)
        total = total + jnp.dot(d_qkv, proj_flat.T, preferred_element_type=jnp.float32)
        qkv_grad = jnp.dot(flat_in.T, d_qkv, preferred_element_type=jnp.float32).reshape(D, 3, HD)
        return (total, (qkv_grad, out_grad))
    start = jnp.zeros((TOKENS, D), jnp.float32)
    total, (qkv_grads, out_grads) = lax.scan(step, start, (head_w, w_out, time_bias))
    root = math.sqrt(TOKENS)
    grad_input = total.astype(jnp.bfloat16).reshape(FRAMES, POS, D)
    grad_qkv = jnp.moveaxis(qkv_grads, 0, 2) / root
    grad_out = out_grads / root
    return (grad_input, grad_qkv, grad_out)
```

```python
import functools
import math

import jax
import jax.numpy as jnp
from jax import lax
from jax.experimental import pallas as pl
from jax.experimental.pallas import tpu as pltpu
from jax.sharding import PartitionSpec as P

BF = jnp.bfloat16
F32 = jnp.float32
STEP = 16
MIB = 1 << 20


def xor_pairs(size, bit):
    return [(i, i ^ bit) for i in range(size)]


def dot(a, b, dims):
    return lax.dot_general(a, b, ((dims[0], dims[1]), ((), ())), preferred_element_type=F32)


def pack_kernel(h_ref, c_ref, m_ref, o_ref):
    for f in range(h_ref.shape[0]):
        o_ref[:, 0, f] = h_ref[f]
        o_ref[:, 1, f] = c_ref[f] * m_ref[f]


def pack(hidden, cot, mask, first, count):
    frames, seq, _, width = hidden.shape
    off = first // STEP
    data = pl.BlockSpec((frames, seq, STEP, width), lambda i: (0, 0, off + i, 0))
    return pl.pallas_call(
        pack_kernel,
        grid=(count // STEP,),
        in_specs=[data, data, pl.BlockSpec((frames, seq, STEP, 1), lambda i: (0, 0, off + i, 0))],
        out_specs=pl.BlockSpec((seq, 2, frames, STEP, width), lambda i: (0, 0, 0, i, 0)),
        out_shape=jax.ShapeDtypeStruct((seq, 2, frames, count, width), BF),
        compiler_params=pltpu.CompilerParams(vmem_limit_bytes=32 * MIB),
        cost_estimate=pl.CostEstimate(
            flops=0, bytes_accessed=8 * frames * seq * count * width, transcendentals=0
        ),
    )(hidden, cot, mask)


def layer_kernel(tp, heads, n_alias, where_ref, *refs):
    pieces = refs[:tp]
    w_ref, wt_ref, wo_ref, bias_ref = refs[tp : tp + 4]
    x_ref, g_ref, dqkv_ref, attn_ref, keep_ref, send_ref = refs[tp + 4 + n_alias : tp + 10 + n_alias]
    qkv_ref, da_ref = refs[tp + 10 + n_alias :]
    me, parity = where_ref[0], where_ref[1]
    rows = x_ref.shape[1]
    part = wt_ref.shape[1] // tp
    seq = pieces[0].shape[0]
    unit = wt_ref.shape[1] // seq
    head = bias_ref.shape[1]
    size = qkv_ref.shape[1] // (3 * heads)
    scale = 1.0 / math.sqrt(size)
    for j in range(tp):
        block = me ^ j
        for i in range(part // unit):
            dest = block * (part // unit) + i
            side = jnp.where(dest % 2 == parity, 1, 0)
            cols = pl.ds(pl.multiple_of((dest // 2) * unit, unit), unit)
            lanes = slice(i * unit, (i + 1) * unit)
            x_ref[side, :, cols] = pieces[j][:, 0, :, :, lanes].reshape(rows, unit)
            g_ref[side, :, cols] = pieces[j][:, 1, :, :, lanes].reshape(rows, unit)
    da_ref[...] = (
        dot(g_ref[0], wo_ref[0], ((1,), (0,))) + dot(g_ref[1], wo_ref[1], ((1,), (0,)))
    ).astype(BF)
    qkv_ref[...] = (
        dot(x_ref[0], w_ref[0], ((1,), (0,))) + dot(x_ref[1], w_ref[1], ((1,), (0,)))
    ).astype(BF)
    for h in range(heads):
        at = [slice((c * heads + h) * size, (c * heads + h + 1) * size) for c in range(3)]
        q, k, v = (qkv_ref[:, a] for a in at)
        da = da_ref[:, at[0]]
        s = dot(q, k, ((1,), (1,))) * scale + bias_ref[h]
        e = jnp.exp(s - jnp.max(s, axis=1, keepdims=True))
        p = e / jnp.sum(e, axis=1, keepdims=True)
        low = p.astype(BF)
        attn_ref[:, at[0]] = dot(low, v, ((1,), (0,))).astype(BF)
        dqkv_ref[:, at[2]] = dot(low, da, ((0,), (0,))).astype(BF)
        dp = dot(da, v, ((1,), (1,)))
        ds = (p * (dp - jnp.sum(p * dp, axis=1, keepdims=True))).astype(BF)
        dqkv_ref[:, at[0]] = (dot(ds, k, ((1,), (0,))) * scale).astype(BF)
        dqkv_ref[:, at[1]] = (dot(ds, q, ((0,), (0,))) * scale).astype(BF)
    grad = dqkv_ref[...]
    for j in range(tp):
        cols = pl.ds(pl.multiple_of((me ^ j) * part, part), part)
        out = send_ref if j % 2 else keep_ref
        val = dot(grad, wt_ref[:, cols], ((1,), (0,)))
        out[j // 2] = val.astype(out.dtype).reshape(out.shape[1:])


def layer(where, pieces, weights, carried, first, total):
    w2, wt, wo2, bias = weights
    tp = len(pieces)
    seq, _, frames, count, part = pieces[0].shape
    width = part * tp
    rows = seq * frames * STEP
    heads = bias.shape[0]
    cols = w2.shape[2]
    model = cols // 3
    off = first // STEP
    tokens = seq * frames * total
    piece = pl.BlockSpec((seq, 2, frames, STEP, part), lambda i, s: (0, 0, 0, i, 0))

    def whole(a):
        return pl.BlockSpec(a.shape, lambda i, s: (0,) * a.ndim, pipeline_mode=pl.Buffered(1))

    half = pl.BlockSpec((2, rows, width // 2), lambda i, s: (0, off + i, 0))

    def line(n):
        return pl.BlockSpec((rows, n), lambda i, s: (off + i, 0))

    back = pl.BlockSpec((tp // 2, seq, frames, STEP, part), lambda i, s: (0, 0, 0, i, 0))
    sds = jax.ShapeDtypeStruct
    n_alias = len(carried)
    work = seq * frames * count
    return pl.pallas_call(
        functools.partial(layer_kernel, tp, heads, n_alias),
        grid_spec=pltpu.PrefetchScalarGridSpec(
            num_scalar_prefetch=1,
            grid=(count // STEP,),
            in_specs=[piece] * tp
            + [whole(a) for a in weights]
            + [pl.BlockSpec(memory_space=pl.ANY)] * n_alias,
            out_specs=[half, half, line(cols), line(model), back, back],
            scratch_shapes=[pltpu.VMEM((rows, cols), BF), pltpu.VMEM((rows, model), BF)],
        ),
        out_shape=[
            sds((2, tokens, width // 2), BF),
            sds((2, tokens, width // 2), BF),
            sds((tokens, cols), BF),
            sds((tokens, model), BF),
            sds((tp // 2, seq, frames, count, part), F32),
            sds((tp // 2, seq, frames, count, part), BF),
        ],
        input_output_aliases={1 + tp + 4 + i: i for i in range(n_alias)},
        compiler_params=pltpu.CompilerParams(vmem_limit_bytes=56 * MIB),
        cost_estimate=pl.CostEstimate(
            flops=2 * work * width * cols * 7 // 3,
            bytes_accessed=14 * MIB + work * width * 12,
            transcendentals=work * rows * heads,
        ),
    )(where, *pieces, *weights, *carried)


def chunks_of(total):
    units = total // STEP
    if units < 4:
        return [STEP] * units
    last = max(1, units // 4)
    a = (units - last + 1) // 2
    return [n * STEP for n in (a, units - last - a, last)]


def exchange_seq(a):
    return lax.all_to_all(a, "seq", split_axis=0, concat_axis=0, tiled=True)


def on_device(seq, tp, hidden_in, cotangent, token_mask, w_qkv, w_out, time_bias):
    frames, places, part = hidden_in.shape
    width = part * tp
    total = places // seq
    heads, size = w_out.shape[0], w_out.shape[1]
    model = heads * size
    outer = seq // 2
    unit = width // seq
    me_s, me_t = lax.axis_index("seq"), lax.axis_index("tp")
    z, y = me_s // 2, me_s % 2
    where = jnp.stack([me_t, y]).astype(jnp.int32)
    root = math.sqrt(seq * frames * places)

    hidden = hidden_in.reshape(frames, seq, total, part)
    cot = cotangent.reshape(frames, seq, total, part)
    mask = token_mask.astype(BF).reshape(frames, seq, total, 1)
    sizes = chunks_of(total)
    starts = [sum(sizes[:k]) for k in range(len(sizes))]
    packed = [pack(hidden, cot, mask, a, n) for a, n in zip(starts, sizes)]

    proj = w_qkv.reshape(width, 3 * model)
    proj_t = proj.T
    out_t = w_out.reshape(model, width).T

    def sides(a):
        a = a.reshape(outer, 2, unit, a.shape[-1])
        pick = [lax.dynamic_index_in_dim(a, i, 1, False) for i in (1 - y, y)]
        return jnp.stack([p.reshape(width // 2, a.shape[-1]) for p in pick])

    place = jnp.arange(STEP)
    same = (place[:, None] == place[None, :])[None, None, :, None, :]
    bias = jnp.where(same, time_bias[:, :, None, :, None], -1e30)
    step_rows = seq * frames * STEP
    weights = (sides(proj), proj_t, sides(out_t), bias.reshape(heads, step_rows, step_rows))

    carried = []
    arrived, outs = [], []
    for k, (a, n) in enumerate(zip(starts, sizes)):
        block = packed[k]
        if k >= 2:
            block, arrived[k - 2] = lax.optimization_barrier((block, arrived[k - 2]))
        block = exchange_seq(block)
        pieces = {0: block}
        bit = tp // 2
        while bit:
            for j in list(pieces):
                pieces[j ^ bit] = lax.ppermute(pieces[j], "tp", xor_pairs(tp, bit))
            bit //= 2
        arrived.append([pieces[j] for j in range(tp)])
    for k, (a, n) in enumerate(zip(starts, sizes)):
        res = layer(where, arrived[k], weights, carried, a, total)
        carried = res[:4]
        keep, send = res[4:]
        bit = 1
        while True:
            got = lax.ppermute(send, "tp", xor_pairs(tp, bit))
            both = keep.astype(F32) + got.astype(F32)
            bit *= 2
            if bit >= tp:
                break
            keep, send = both[0::2], both[1::2].astype(BF)
        outs.append(exchange_seq(both[0].astype(BF)))
    x2, g2, dqkv, attn = carried

    def summed(lhs, rhs):
        def rows_of(side):
            return dot(lhs[side], rhs, ((0,), (0,))).astype(BF)

        got = lax.ppermute(rows_of(0), "seq", xor_pairs(seq, 1))
        both = (rows_of(1).astype(F32) + got.astype(F32)).astype(BF).reshape(outer, unit, rhs.shape[1])
        groups = [[2 * i + b for i in range(outer)] for b in range(2)]
        parts = lax.all_to_all(
            both, "seq", split_axis=0, concat_axis=0, tiled=True, axis_index_groups=groups
        )
        return jnp.sum(parts.astype(F32), axis=0) / root

    out_sum = summed(g2, attn).T.reshape(heads, size, unit)
    cols = [summed(x2, dqkv[:, c * model : (c + 1) * model]) for c in (2, 1, 0)]
    grad_qkv = jnp.concatenate(cols[::-1], axis=1).reshape(unit, 3, heads, size)
    grad_input = jnp.concatenate([jnp.swapaxes(o, 0, 1) for o in outs], axis=2).reshape(
        frames, places, part
    )
    return (grad_input, grad_qkv, out_sum)


def solution(mesh):
    in_specs = (
        P("seq", None, "tp"),
        P("seq", None, "tp"),
        P("seq", None),
        P(None, None, "tp", None),
        P("tp", None, None),
        P("tp", None, None),
    )
    out_specs = (P("seq", None, "tp"), P("seq", None, "tp", None), P("tp", None, "seq"))
    return jax.shard_map(
        functools.partial(on_device, mesh.shape["seq"], mesh.shape["tp"]),
        mesh=mesh,
        in_specs=in_specs,
        out_specs=out_specs,
        check_vma=False,
    )
```

```python
import functools
import math

import jax
import jax.numpy as jnp
from jax import lax
from jax.experimental import pallas as pl
from jax.experimental.pallas import tpu as pltpu
from jax.sharding import PartitionSpec as P

BF = jnp.bfloat16
F32 = jnp.float32
STEP = 16
MIB = 1 << 20


def xor_pairs(size, bit):
    return [(i, i ^ bit) for i in range(size)]


def dot(a, b, dims):
    return lax.dot_general(a, b, ((dims[0], dims[1]), ((), ())), preferred_element_type=F32)


def pack_kernel(h_ref, c_ref, m_ref, o_ref):
    for f in range(h_ref.shape[0]):
        o_ref[:, 0, f] = h_ref[f]
        o_ref[:, 1, f] = c_ref[f] * m_ref[f]


def pack(hidden, cot, mask, first, count):
    frames, seq, _, width = hidden.shape
    off = first // STEP
    data = pl.BlockSpec((frames, seq, STEP, width), lambda i: (0, 0, off + i, 0))
    return pl.pallas_call(
        pack_kernel,
        grid=(count // STEP,),
        in_specs=[data, data, pl.BlockSpec((frames, seq, STEP, 1), lambda i: (0, 0, off + i, 0))],
        out_specs=pl.BlockSpec((seq, 2, frames, STEP, width), lambda i: (0, 0, 0, i, 0)),
        out_shape=jax.ShapeDtypeStruct((seq, 2, frames, count, width), BF),
        compiler_params=pltpu.CompilerParams(vmem_limit_bytes=32 * MIB),
        cost_estimate=pl.CostEstimate(
            flops=0, bytes_accessed=8 * frames * seq * count * width, transcendentals=0
        ),
    )(hidden, cot, mask)


def layer_kernel(tp, heads, n_alias, where_ref, *refs):
    pieces = refs[:tp]
    w_ref, wo_ref, line_ref = refs[tp : tp + 3]
    outs = refs[tp + 3 + n_alias : -6]
    x_ref, g_ref, dq_ref, dk_ref, dv_ref, attn_ref, send_ref = outs[:7]
    keep_refs = outs[7:]
    qkv_ref, da_ref, bias_ref, dqkv_ref, xall_ref, gall_ref = refs[-6:]
    me, parity = where_ref[0], where_ref[1]
    rows = x_ref.shape[1]
    seq = pieces[0].shape[0]
    part = pieces[0].shape[-1]
    unit = part * tp // seq
    size = qkv_ref.shape[1] // (3 * heads)
    scale = 1.0 / math.sqrt(size)

    @pl.when(pl.program_id(0) == 0)
    def _():
        at = [lax.broadcasted_iota(jnp.int32, (rows, rows), d) % STEP for d in range(2)]
        for h in range(heads):
            wide = jnp.broadcast_to(line_ref[h][:, None, :], (rows // STEP, STEP, rows))
            bias_ref[h] = jnp.where(at[0] == at[1], wide.reshape(rows, rows), -1e30)

    for j in range(tp):
        block = me ^ j
        xs = pieces[j][:, 0].reshape(rows, part)
        gs = pieces[j][:, 1].reshape(rows, part)
        cols = pl.ds(pl.multiple_of(block * part, part), part)
        xall_ref[:, cols] = xs
        gall_ref[:, cols] = gs
        for i in range(part // unit):
            dest = block * (part // unit) + i
            side = jnp.where(dest % 2 == parity, 1, 0)
            cols = pl.ds(pl.multiple_of((dest // 2) * unit, unit), unit)
            lanes = slice(i * unit, (i + 1) * unit)
            x_ref[side, :, cols] = xs[:, lanes]
            g_ref[side, :, cols] = gs[:, lanes]
    da_ref[...] = dot(gall_ref[...], wo_ref[...], ((1,), (1,))).astype(BF)
    qkv_ref[...] = dot(xall_ref[...], w_ref[...], ((1,), (0,))).astype(BF)
    for h in range(heads):
        at = [slice((c * heads + h) * size, (c * heads + h + 1) * size) for c in range(3)]
        q, k, v = (qkv_ref[:, a] for a in at)
        da = da_ref[:, at[0]]
        s = dot(q, k, ((1,), (1,))) * scale + bias_ref[h]
        e = jnp.exp(s - jnp.max(s, axis=1, keepdims=True))
        p = e / jnp.sum(e, axis=1, keepdims=True)
        low = p.astype(BF)
        attn_ref[:, at[0]] = dot(low, v, ((1,), (0,))).astype(BF)
        dv = dot(low, da, ((0,), (0,))).astype(BF)
        dp = dot(da, v, ((1,), (1,)))
        ds = (p * (dp - jnp.sum(p * dp, axis=1, keepdims=True))).astype(BF)
        dq = (dot(ds, k, ((1,), (0,))) * scale).astype(BF)
        dk = (dot(ds, q, ((0,), (0,))) * scale).astype(BF)
        for a, out, val in zip(at, (dq_ref, dk_ref, dv_ref), (dq, dk, dv)):
            dqkv_ref[:, a] = val
            out[:, at[0]] = val
    grad = dqkv_ref[...]
    for j in range(tp):
        cols = pl.ds(pl.multiple_of((me ^ j) * part, part), part)
        val = dot(grad, w_ref[cols, :], ((1,), (1,)))
        if j % 2:
            send_ref[j // 2] = val.astype(BF).reshape(send_ref.shape[1:])
        else:
            keep_refs[j // 2][...] = val.reshape(send_ref.shape[1:])


def layer(where, pieces, weights, carried, first, total):
    w, _, bias = weights
    tp = len(pieces)
    seq, _, frames, count, part = pieces[0].shape
    width = part * tp
    rows = seq * frames * STEP
    heads = bias.shape[0]
    cols = w.shape[1]
    model = cols // 3
    off = first // STEP
    tokens = seq * frames * total
    piece = pl.BlockSpec((seq, 2, frames, STEP, part), lambda i, s: (0, 0, 0, i, 0))

    def whole(a):
        return pl.BlockSpec(a.shape, lambda i, s: (0,) * a.ndim, pipeline_mode=pl.Buffered(1))

    half = pl.BlockSpec((2, rows, width // 2), lambda i, s: (0, off + i, 0))

    def line(n):
        return pl.BlockSpec((rows, n), lambda i, s: (off + i, 0))

    back = pl.BlockSpec((tp // 2, seq, frames, STEP, part), lambda i, s: (0, 0, 0, i, 0))
    stay = pl.BlockSpec((seq, frames, STEP, part), lambda i, s: (0, 0, i, 0))
    sds = jax.ShapeDtypeStruct
    n_alias = len(carried)
    work = seq * frames * count
    return pl.pallas_call(
        functools.partial(layer_kernel, tp, heads, n_alias),
        grid_spec=pltpu.PrefetchScalarGridSpec(
            num_scalar_prefetch=1,
            grid=(count // STEP,),
            in_specs=[piece] * tp
            + [whole(a) for a in weights]
            + [pl.BlockSpec(memory_space=pl.ANY)] * n_alias,
            out_specs=[half, half] + [line(model)] * 4 + [back] + [stay] * (tp // 2),
            scratch_shapes=[
                pltpu.VMEM((rows, cols), BF),
                pltpu.VMEM((rows, model), BF),
                pltpu.VMEM((heads, rows, rows), F32),
                pltpu.VMEM((rows, cols), BF),
                pltpu.VMEM((rows, width), BF),
                pltpu.VMEM((rows, width), BF),
            ],
        ),
        out_shape=[
            sds((2, tokens, width // 2), BF),
            sds((2, tokens, width // 2), BF),
            *[sds((tokens, model), BF)] * 4,
            sds((tp // 2, seq, frames, count, part), BF),
            *[sds((seq, frames, count, part), F32)] * (tp // 2),
        ],
        input_output_aliases={1 + tp + 3 + i: i for i in range(n_alias)},
        compiler_params=pltpu.CompilerParams(vmem_limit_bytes=56 * MIB),
        cost_estimate=pl.CostEstimate(
            flops=2 * work * width * cols * 7 // 3,
            bytes_accessed=8 * MIB + work * width * 12,
            transcendentals=work * rows * heads,
        ),
    )(where, *pieces, *weights, *carried)


def chunks_of(total):
    units = total // STEP
    parts = 4 if units % 4 == 0 else units
    return [units // parts * STEP] * parts


def exchange_seq(a):
    return lax.all_to_all(a, "seq", split_axis=0, concat_axis=0, tiled=True)


def on_device(seq, tp, hidden_in, cotangent, token_mask, w_qkv, w_out, time_bias):
    frames, places, part = hidden_in.shape
    width = part * tp
    total = places // seq
    heads, size = w_out.shape[0], w_out.shape[1]
    model = heads * size
    outer = seq // 2
    unit = width // seq
    me_s, me_t = lax.axis_index("seq"), lax.axis_index("tp")
    z, y = me_s // 2, me_s % 2
    where = jnp.stack([me_t, y]).astype(jnp.int32)
    root = math.sqrt(seq * frames * places)

    hidden = hidden_in.reshape(frames, seq, total, part)
    cot = cotangent.reshape(frames, seq, total, part)
    mask = token_mask.astype(BF).reshape(frames, seq, total, 1)
    sizes = chunks_of(total)
    starts = [sum(sizes[:k]) for k in range(len(sizes))]
    packed = [pack(hidden, cot, mask, a, n) for a, n in zip(starts, sizes)]

    step_rows = seq * frames * STEP
    lines = jnp.broadcast_to(time_bias[..., None], time_bias.shape + (STEP,))
    weights = (
        w_qkv.reshape(width, 3 * model),
        w_out.reshape(model, width),
        lines.reshape(heads, seq * frames, step_rows),
    )

    def tie(a, *others):
        return lax.optimization_barrier((a, *others))[0]

    blocks, crossed = [], []
    packed[1], weights = lax.optimization_barrier((packed[1], weights))
    for k in range(len(sizes)):
        block = packed[k]
        if k >= 2:
            block = tie(block, crossed[k - 2])
        blocks.append(exchange_seq(block))
        if k == 0:
            blocks[0], weights = lax.optimization_barrier((blocks[0], weights))
        crossed.append(lax.ppermute(blocks[k], "tp", xor_pairs(tp, tp // 2)))

    def near(k):
        pieces = {0: blocks[k], tp // 2: crossed[k]}
        bit = tp // 4
        while bit:
            for j in list(pieces):
                pieces[j ^ bit] = lax.ppermute(pieces[j], "tp", xor_pairs(tp, bit))
            bit //= 2
        return [pieces[j] for j in range(tp)]

    def reduced(keep, send):
        bit = 1
        while True:
            got = lax.ppermute(send, "tp", xor_pairs(tp, bit))
            keep = [a + got[m].astype(F32) for m, a in enumerate(keep)]
            bit *= 2
            if 2 * bit > tp:
                return keep, send
            send = jnp.stack([a.astype(BF) for a in keep[1::2]])
            if 2 * bit == tp:
                return keep[0], send
            keep = keep[0::2]

    carried, local, sent = [], [], []
    outs, homes = [], []

    def across(first, last):
        return lax.ppermute(
            jnp.concatenate(sent[first:last], axis=3), "tp", xor_pairs(tp, tp // 2)
        )

    def send_home(first, last, got, *ready):
        got = tie(got, *ready) if ready else got
        keep = jnp.concatenate(local[first:last], axis=2)
        outs.append((keep + got[0].astype(F32)).astype(BF))
        homes.append(exchange_seq(tie(outs[-1], *homes[-1:])))

    for k, a in enumerate(starts):
        pieces = near(k)
        if k == len(starts) - 1:
            far = across(0, k)
            carried[0] = tie(carried[0], sent[k - 1])
        res = list(layer(where, pieces, weights, carried, a, total))
        carried = res[:6]
        if k + 1 < len(sizes):
            crossed[k + 1] = tie(crossed[k + 1], carried[5])
        keep, send = reduced(res[7:], res[6])
        local.append(keep)
        sent.append(send)

    x2, g2, dq, dk, dv, attn = carried

    last = [attn]

    def weight_rows(lhs, side, rhs):
        rhs, last[0] = lax.optimization_barrier((rhs, last[0]))
        last[0] = dot(lhs[side], rhs, ((0,), (0,))).astype(BF)
        return last[0]

    bits = [(z >> b) & 1 for b in range(outer.bit_length() - 1)]

    def swap(keep, send, bit, final=False):
        got = lax.ppermute(send, "seq", xor_pairs(seq, bit))
        both = keep.astype(F32) + got.astype(F32)
        return both / root if final else both.astype(BF)

    def halves(a, axis, b):
        pick = [lax.dynamic_index_in_dim(a, i, axis, False) for i in (bits[b], 1 - bits[b])]
        return pick[0], pick[1]

    def along_z(a, todo, axis):
        for n, b in enumerate(todo):
            keep, send = halves(a, axis + len(todo) - 1 - n, b)
            a = swap(keep, send, 2 << b, n == len(todo) - 1)
        return a

    nbits = len(bits)
    cube = (2,) * nbits + (unit, model)
    every = list(range(nbits))

    def first_z(sides_of):
        keep, send = halves(jnp.stack([p.reshape(cube) for p in sides_of]), nbits, 0)
        return swap(keep, send, 2)

    n = len(sizes) - 1
    send_o = weight_rows(g2, 0, attn)
    both_v = [weight_rows(x2, side, dv) for side in range(2)]
    send_k = weight_rows(x2, 0, dk)
    send_home(0, n, far, send_k)
    send_q = weight_rows(x2, 0, dq)
    keep_o = weight_rows(g2, 1, attn)
    keep_k = weight_rows(x2, 1, tie(dk, sent[-1]))
    keep_q = weight_rows(x2, 1, dq)
    sum_o = swap(keep_o, send_o, 1)
    sent[n] = tie(sent[n], outs[0])
    send_home(n, n + 1, across(n, n + 1))
    sum_v = first_z(both_v)
    sum_k = swap(keep_k, send_k, 1)
    sum_q = swap(keep_q, tie(send_q, sum_o), 1)
    out_sum = along_z(sum_o.reshape(cube), every, 0).T.reshape(heads, size, unit)
    sum_v = along_z(swap(sum_v[1], sum_v[0], 1, nbits == 1), every[1:], 0)
    sum_k = along_z(tie(sum_k, homes[-2]).reshape(cube), every, 0)
    sum_q = along_z(tie(sum_q, homes[-1]).reshape(cube), every, 0)
    grad_qkv = jnp.concatenate([sum_q, sum_k, sum_v], axis=1).reshape(unit, 3, heads, size)
    grad_input = jnp.concatenate([jnp.swapaxes(o, 0, 1) for o in homes], axis=2).reshape(
        frames, places, part
    )
    return (grad_input, grad_qkv, out_sum)


def solution(mesh):
    in_specs = (
        P("seq", None, "tp"),
        P("seq", None, "tp"),
        P("seq", None),
        P(None, None, "tp", None),
        P("tp", None, None),
        P("tp", None, None),
    )
    out_specs = (P("seq", None, "tp"), P("seq", None, "tp", None), P("tp", None, "seq"))
    return jax.shard_map(
        functools.partial(on_device, mesh.shape["seq"], mesh.shape["tp"]),
        mesh=mesh,
        in_specs=in_specs,
        out_specs=out_specs,
        check_vma=False,
    )
```

```python
import functools
import math

import jax
import jax.numpy as jnp
from jax import lax
from jax.experimental import pallas as pl
from jax.experimental.pallas import tpu as pltpu
from jax.sharding import PartitionSpec as P

BF = jnp.bfloat16
F32 = jnp.float32
STEP = 16
MIB = 1 << 20


def xor_pairs(size, bit):
    return [(i, i ^ bit) for i in range(size)]


def dot(a, b, dims):
    return lax.dot_general(a, b, ((dims[0], dims[1]), ((), ())), preferred_element_type=F32)


def pack_kernel(h_ref, c_ref, m_ref, o_ref):
    for f in range(h_ref.shape[0]):
        o_ref[:, 0, f] = h_ref[f]
        o_ref[:, 1, f] = c_ref[f] * m_ref[f]


def pack(hidden, cot, mask, first, count):
    frames, seq, _, width = hidden.shape
    off = first // STEP
    data = pl.BlockSpec((frames, seq, STEP, width), lambda i: (0, 0, off + i, 0))
    return pl.pallas_call(
        pack_kernel,
        grid=(count // STEP,),
        in_specs=[data, data, pl.BlockSpec((frames, seq, STEP, 1), lambda i: (0, 0, off + i, 0))],
        out_specs=pl.BlockSpec((seq, 2, frames, STEP, width), lambda i: (0, 0, 0, i, 0)),
        out_shape=jax.ShapeDtypeStruct((seq, 2, frames, count, width), BF),
        compiler_params=pltpu.CompilerParams(vmem_limit_bytes=32 * MIB),
        cost_estimate=pl.CostEstimate(
            flops=0, bytes_accessed=8 * frames * seq * count * width, transcendentals=0
        ),
    )(hidden, cot, mask)


def layer_kernel(tp, heads, n_alias, where_ref, *refs):
    pieces = refs[:tp]
    w_ref, wo_ref, line_ref = refs[tp : tp + 3]
    outs = refs[tp + 3 + n_alias : -6]
    x_ref, g_ref, dq_ref, dk_ref, dv_ref, attn_ref, send_ref = outs[:7]
    keep_refs = outs[7:]
    qkv_ref, da_ref, bias_ref, dqkv_ref, xall_ref, gall_ref = refs[-6:]
    me, parity = where_ref[0], where_ref[1]
    rows = x_ref.shape[1]
    seq = pieces[0].shape[0]
    part = pieces[0].shape[-1]
    unit = part * tp // seq
    size = qkv_ref.shape[1] // (3 * heads)
    scale = 1.0 / math.sqrt(size)

    @pl.when(pl.program_id(0) == 0)
    def _():
        at = [lax.broadcasted_iota(jnp.int32, (rows, rows), d) % STEP for d in range(2)]
        for h in range(heads):
            wide = jnp.broadcast_to(line_ref[h][:, None, :], (rows // STEP, STEP, rows))
            bias_ref[h] = jnp.where(at[0] == at[1], wide.reshape(rows, rows), -1e30)

    for j in range(tp):
        block = me ^ j
        xs = pieces[j][:, 0].reshape(rows, part)
        gs = pieces[j][:, 1].reshape(rows, part)
        cols = pl.ds(pl.multiple_of(block * part, part), part)
        xall_ref[:, cols] = xs
        gall_ref[:, cols] = gs
        for i in range(part // unit):
            dest = block * (part // unit) + i
            side = jnp.where(dest % 2 == parity, 1, 0)
            cols = pl.ds(pl.multiple_of((dest // 2) * unit, unit), unit)
            lanes = slice(i * unit, (i + 1) * unit)
            x_ref[side, :, cols] = xs[:, lanes]
            g_ref[side, :, cols] = gs[:, lanes]
    da_ref[...] = dot(gall_ref[...], wo_ref[...], ((1,), (1,))).astype(BF)
    qkv_ref[...] = dot(xall_ref[...], w_ref[...], ((1,), (0,))).astype(BF)
    for h in range(heads):
        at = [slice((c * heads + h) * size, (c * heads + h + 1) * size) for c in range(3)]
        q, k, v = (qkv_ref[:, a] for a in at)
        da = da_ref[:, at[0]]
        s = dot(q, k, ((1,), (1,))) * scale + bias_ref[h]
        e = jnp.exp(s - jnp.max(s, axis=1, keepdims=True))
        p = e / jnp.sum(e, axis=1, keepdims=True)
        low = p.astype(BF)
        attn_ref[:, at[0]] = dot(low, v, ((1,), (0,))).astype(BF)
        dv = dot(low, da, ((0,), (0,))).astype(BF)
        dp = dot(da, v, ((1,), (1,)))
        ds = (p * (dp - jnp.sum(p * dp, axis=1, keepdims=True))).astype(BF)
        dq = (dot(ds, k, ((1,), (0,))) * scale).astype(BF)
        dk = (dot(ds, q, ((0,), (0,))) * scale).astype(BF)
        for a, out, val in zip(at, (dq_ref, dk_ref, dv_ref), (dq, dk, dv)):
            dqkv_ref[:, a] = val
            out[:, at[0]] = val
    grad = dqkv_ref[...]
    for j in range(tp):
        cols = pl.ds(pl.multiple_of((me ^ j) * part, part), part)
        val = dot(grad, w_ref[cols, :], ((1,), (1,)))
        if j % 2:
            send_ref[j // 2] = val.astype(BF).reshape(send_ref.shape[1:])
        else:
            keep_refs[j // 2][...] = val.reshape(send_ref.shape[1:])


def layer(where, pieces, weights, carried, first, total):
    w, _, bias = weights
    tp = len(pieces)
    seq, _, frames, count, part = pieces[0].shape
    width = part * tp
    rows = seq * frames * STEP
    heads = bias.shape[0]
    cols = w.shape[1]
    model = cols // 3
    off = first // STEP
    tokens = seq * frames * total
    piece = pl.BlockSpec((seq, 2, frames, STEP, part), lambda i, s: (0, 0, 0, i, 0))

    def whole(a):
        return pl.BlockSpec(a.shape, lambda i, s: (0,) * a.ndim, pipeline_mode=pl.Buffered(1))

    half = pl.BlockSpec((2, rows, width // 2), lambda i, s: (0, off + i, 0))

    def line(n):
        return pl.BlockSpec((rows, n), lambda i, s: (off + i, 0))

    back = pl.BlockSpec((tp // 2, seq, frames, STEP, part), lambda i, s: (0, 0, 0, i, 0))
    stay = pl.BlockSpec((seq, frames, STEP, part), lambda i, s: (0, 0, i, 0))
    sds = jax.ShapeDtypeStruct
    n_alias = len(carried)
    work = seq * frames * count
    return pl.pallas_call(
        functools.partial(layer_kernel, tp, heads, n_alias),
        grid_spec=pltpu.PrefetchScalarGridSpec(
            num_scalar_prefetch=1,
            grid=(count // STEP,),
            in_specs=[piece] * tp
            + [whole(a) for a in weights]
            + [pl.BlockSpec(memory_space=pl.ANY)] * n_alias,
            out_specs=[half, half] + [line(model)] * 4 + [back] + [stay] * (tp // 2),
            scratch_shapes=[
                pltpu.VMEM((rows, cols), BF),
                pltpu.VMEM((rows, model), BF),
                pltpu.VMEM((heads, rows, rows), F32),
                pltpu.VMEM((rows, cols), BF),
                pltpu.VMEM((rows, width), BF),
                pltpu.VMEM((rows, width), BF),
            ],
        ),
        out_shape=[
            sds((2, tokens, width // 2), BF),
            sds((2, tokens, width // 2), BF),
            *[sds((tokens, model), BF)] * 4,
            sds((tp // 2, seq, frames, count, part), BF),
            *[sds((seq, frames, count, part), F32)] * (tp // 2),
        ],
        input_output_aliases={1 + tp + 3 + i: i for i in range(n_alias)},
        compiler_params=pltpu.CompilerParams(vmem_limit_bytes=56 * MIB),
        cost_estimate=pl.CostEstimate(
            flops=2 * work * width * cols * 7 // 3,
            bytes_accessed=8 * MIB + work * width * 12,
            transcendentals=work * rows * heads,
        ),
    )(where, *pieces, *weights, *carried)


def chunks_of(total):
    units = total // STEP
    parts = 4 if units % 4 == 0 else units
    return [units // parts * STEP] * parts


def exchange_seq(a):
    return lax.all_to_all(a, "seq", split_axis=0, concat_axis=0, tiled=True)


def on_device(seq, tp, hidden_in, cotangent, token_mask, w_qkv, w_out, time_bias):
    frames, places, part = hidden_in.shape
    width = part * tp
    total = places // seq
    heads, size = w_out.shape[0], w_out.shape[1]
    model = heads * size
    outer = seq // 2
    unit = width // seq
    me_s, me_t = lax.axis_index("seq"), lax.axis_index("tp")
    z, y = me_s // 2, me_s % 2
    where = jnp.stack([me_t, y]).astype(jnp.int32)
    root = math.sqrt(seq * frames * places)

    hidden = hidden_in.reshape(frames, seq, total, part)
    cot = cotangent.reshape(frames, seq, total, part)
    mask = token_mask.astype(BF).reshape(frames, seq, total, 1)
    sizes = chunks_of(total)
    starts = [sum(sizes[:k]) for k in range(len(sizes))]
    packed = [pack(hidden, cot, mask, a, n) for a, n in zip(starts, sizes)]

    step_rows = seq * frames * STEP
    lines = jnp.broadcast_to(time_bias[..., None], time_bias.shape + (STEP,))
    weights = (
        w_qkv.reshape(width, 3 * model),
        w_out.reshape(model, width),
        lines.reshape(heads, seq * frames, step_rows),
    )

    def tie(a, *others):
        return lax.optimization_barrier((a, *others))[0]

    blocks, crossed = [], []
    packed[1], weights = lax.optimization_barrier((packed[1], weights))
    for k in range(len(sizes)):
        block = packed[k]
        if k >= 2:
            block = tie(block, crossed[k - 2])
        blocks.append(exchange_seq(block))
        if k == 0:
            blocks[0], weights = lax.optimization_barrier((blocks[0], weights))
        crossed.append(lax.ppermute(blocks[k], "tp", xor_pairs(tp, tp // 2)))

    def near(k):
        pieces = {0: blocks[k], tp // 2: crossed[k]}
        bit = tp // 4
        while bit:
            for j in list(pieces):
                pieces[j ^ bit] = lax.ppermute(pieces[j], "tp", xor_pairs(tp, bit))
            bit //= 2
        return [pieces[j] for j in range(tp)]

    def reduced(keep, send):
        bit = 1
        while True:
            got = lax.ppermute(send, "tp", xor_pairs(tp, bit))
            keep = [a + got[m].astype(F32) for m, a in enumerate(keep)]
            bit *= 2
            if 2 * bit > tp:
                return keep, send
            send = jnp.stack([a.astype(BF) for a in keep[1::2]])
            if 2 * bit == tp:
                return keep[0], send
            keep = keep[0::2]

    carried, local, sent = [], [], []
    outs, homes = [], []

    def across(first, last):
        return jnp.concatenate(sent[first:last], axis=3)

    def send_home(first, last, far, *ready):
        got = lax.ppermute(far, "tp", xor_pairs(tp, tp // 2))
        got = tie(got, *ready) if ready else got
        keep = jnp.concatenate(local[first:last], axis=2)
        outs.append((keep + got[0].astype(F32)).astype(BF))
        homes.append(exchange_seq(tie(outs[-1], *homes[-1:])))

    for k, a in enumerate(starts):
        pieces = near(k)
        if k == len(starts) - 1:
            far = across(0, k)
            carried[0] = tie(carried[0], far)
        res = list(layer(where, pieces, weights, carried, a, total))
        carried = res[:6]
        if k + 1 < len(sizes):
            crossed[k + 1] = tie(crossed[k + 1], carried[5])
        keep, send = reduced(res[7:], res[6])
        local.append(keep)
        sent.append(send)

    x2, g2, dq, dk, dv, attn = carried

    last = [attn]

    def weight_rows(lhs, side, rhs):
        rhs, last[0] = lax.optimization_barrier((rhs, last[0]))
        last[0] = dot(lhs[side], rhs, ((0,), (0,))).astype(BF)
        return last[0]

    bits = [(z >> b) & 1 for b in range(outer.bit_length() - 1)]

    def swap(keep, send, bit, final=False):
        got = lax.ppermute(send, "seq", xor_pairs(seq, bit))
        both = keep.astype(F32) + got.astype(F32)
        return both / root if final else both.astype(BF)

    def halves(a, axis, b):
        pick = [lax.dynamic_index_in_dim(a, i, axis, False) for i in (bits[b], 1 - bits[b])]
        return pick[0], pick[1]

    def along_z(a, todo, axis):
        for n, b in enumerate(todo):
            keep, send = halves(a, axis + len(todo) - 1 - n, b)
            a = swap(keep, send, 2 << b, n == len(todo) - 1)
        return a

    nbits = len(bits)
    cube = (2,) * nbits + (unit, model)
    every = list(range(nbits))

    def first_z(sides_of):
        keep, send = halves(jnp.stack([p.reshape(cube) for p in sides_of]), nbits, 0)
        return swap(keep, send, 2)

    n = len(sizes) - 1
    send_o = weight_rows(g2, 0, attn)
    both_v = [weight_rows(x2, side, dv) for side in range(2)]
    send_k = weight_rows(x2, 0, dk)
    send_home(0, n, far, send_o)
    send_q = weight_rows(x2, 0, dq)
    keep_o = weight_rows(g2, 1, tie(attn, outs[0]))
    keep_k = weight_rows(x2, 1, tie(dk, sent[-1]))
    keep_q = weight_rows(x2, 1, dq)
    sum_o = swap(keep_o, send_o, 1)
    sent[n] = tie(sent[n], outs[0])
    send_home(n, n + 1, across(n, n + 1))
    sum_v = first_z(both_v)
    sum_k = swap(keep_k, send_k, 1)
    sum_q = swap(keep_q, tie(send_q, sum_o), 1)
    out_sum = along_z(tie(sum_o, homes[0]).reshape(cube), every, 0).T.reshape(heads, size, unit)
    sum_v = along_z(swap(sum_v[1], sum_v[0], 1, nbits == 1), every[1:], 0)
    sum_k = along_z(sum_k.reshape(cube), every, 0)
    sum_q = along_z(tie(sum_q, homes[-1]).reshape(cube), every, 0)
    grad_qkv = jnp.concatenate([sum_q, sum_k, sum_v], axis=1).reshape(unit, 3, heads, size)
    grad_input = jnp.concatenate([jnp.swapaxes(o, 0, 1) for o in homes], axis=2).reshape(
        frames, places, part
    )
    return (grad_input, grad_qkv, out_sum)


def solution(mesh):
    in_specs = (
        P("seq", None, "tp"),
        P("seq", None, "tp"),
        P("seq", None),
        P(None, None, "tp", None),
        P("tp", None, None),
        P("tp", None, None),
    )
    out_specs = (P("seq", None, "tp"), P("seq", None, "tp", None), P("tp", None, "seq"))
    return jax.shard_map(
        functools.partial(on_device, mesh.shape["seq"], mesh.shape["tp"]),
        mesh=mesh,
        in_specs=in_specs,
        out_specs=out_specs,
        check_vma=False,
    )
```
